256 devices in a mesh: rows: 32 (over y_hi, z, core), cols: 8 (over y_lo, x).
Axes of the slice: x: 4, y: 4 (y_hi: 2, y_lo: 2; y = y_hi * 2 + y_lo), z: 8, core: 2. Of those that a mesh axis runs over, the one named last changes fastest.
Arguments:
- grid: bfloat16 [512, 512, 512], P('rows', 'cols'), may hold values from -9 to 9
- gain_lon: float32 [512], replicated, may hold values from 0.25 to 1.75
- qkv_lon: bfloat16 [512, 1536], replicated, may hold values from -1 to 1
- out_lon: bfloat16 [512, 512], replicated, may hold values from -0.25 to 0.25
- gain_lat: float32 [512], replicated, may hold values from 0.25 to 1.75
- qkv_lat: bfloat16 [512, 1536], replicated, may hold values from -1 to 1
- out_lat: bfloat16 [512, 512], replicated, may hold values from -0.25 to 0.25
Outputs:
- updated: bfloat16 [512, 512, 512], P('rows', 'cols')
The draws below stay inside these ranges and needn't reach their ends.
All inputs are finite; a program needn't handle non-finite values.
Results may differ from the reference program's by a relative error of at most 0.009.
Values may be sent and summed in bfloat16 or wider, within the bound.
A program may use at most 64 MiB of HBM per device.

```python
import jax
import jax.numpy as jnp
from jax import lax

D = 512
HEADS = 8
HD = 64
H = 512
W = 512


def draw_grid(key, part):
    own_key = jax.random.fold_in(key, 103)
    random_part = jax.random.truncated_normal(own_key, -6.0, 6.0, (H, W, D), jnp.float32)
    return random_part.astype(jnp.bfloat16)


def draw_qkv_lon(key, part):
    own_key = jax.random.fold_in(key, 101)
    random_part = jax.random.truncated_normal(own_key, -6.0, 6.0, (D, 3 * D), jnp.float32) * D ** (-0.5)
    return random_part.astype(jnp.bfloat16)


def draw_qkv_lat(key, part):
    own_key = jax.random.fold_in(key, 102)
    random_part = jax.random.truncated_normal(own_key, -6.0, 6.0, (D, 3 * D), jnp.float32) * D ** (-0.5)
    return random_part.astype(jnp.bfloat16)


def centred(key, dims, deviation, reach, kind=jnp.bfloat16):
    return jnp.clip(deviation * jax.random.normal(key, dims, jnp.float32), -reach, reach).astype(kind)


def setup_inputs(seed: int = 0) -> dict:
    key_list = jax.random.split(jax.random.key(seed), 8)
    grid = draw_grid(jax.random.fold_in(key_list[7], 71), 0)
    gain_lon = jnp.clip(1.0 + 0.15 * jax.random.normal(key_list[1], (D,), jnp.float32), 0.25, 1.75)
    qkv_lon = draw_qkv_lon(jax.random.fold_in(key_list[7], 71), 0)
    out_lon = centred(key_list[3], (D, D), D ** -0.5, 0.25)
    gain_lat = jnp.clip(1.0 + 0.15 * jax.random.normal(key_list[4], (D,), jnp.float32), 0.25, 1.75)
    qkv_lat = draw_qkv_lat(jax.random.fold_in(key_list[7], 71), 0)
    out_lat = centred(key_list[6], (D, D), D ** -0.5, 0.25)
    return dict(grid=grid, gain_lon=gain_lon, qkv_lon=qkv_lon, out_lon=out_lon, gain_lat=gain_lat, qkv_lat=qkv_lat, out_lat=out_lat)


def norm_rows(u, gain):
    values = u.astype(jnp.float32)
    scale = lax.rsqrt(lax.optimization_barrier(jnp.mean(values * values, axis=-1, keepdims=True)) + 1e-06)
    return (values * scale * gain).astype(jnp.bfloat16)

def sublayer(line, gain, w_qkv, w_out):
    normed = norm_rows(line, gain)
    proj = jnp.dot(normed, w_qkv, preferred_element_type=jnp.float32).astype(jnp.bfloat16)
    length = line.shape[0]
    query = proj[:, :D].astype(jnp.float32).reshape(length, HEADS, HD)
    keys = proj[:, D:2 * D].astype(jnp.float32).reshape(length, HEADS, HD)
    values = proj[:, 2 * D:].astype(jnp.float32).reshape(length, HEADS, HD)
    scores = jnp.einsum('qhd,khd->hqk', query, keys) * HD ** (-0.5)
    weights = jax.nn.softmax(scores, axis=-1).astype(jnp.bfloat16)
    mixed = jnp.einsum('hqk,khd->qhd', weights.astype(jnp.float32), values).astype(jnp.bfloat16)
    mixed = mixed.reshape(length, D)
    total = line.astype(jnp.float32) + jnp.dot(mixed, w_out, preferred_element_type=jnp.float32)
    return total.astype(jnp.bfloat16)

def reference(grid, gain_lon, qkv_lon, out_lon, gain_lat, qkv_lat, out_lat):
    first = lax.map(lambda line: sublayer(line, gain_lon, qkv_lon, out_lon), grid)
    turned = jnp.transpose(first, (1, 0, 2))
    second = lax.map(lambda line: sublayer(line, gain_lat, qkv_lat, out_lat), turned)
    return jnp.transpose(second, (1, 0, 2))
```

```python
import functools

import jax
import jax.numpy as jnp
from jax import lax
from jax.experimental import pallas as pl
from jax.experimental.pallas import tpu as pltpu
from jax.sharding import PartitionSpec as P

D = 512
PAIRS = 4
SEQ = 512
ROWS = 32
COLS = 8
QB = 128
SCALE = 64 ** (-0.5) * 1.4426950408889634
MESH = pl.DeviceIdType.MESH
BF16 = jnp.bfloat16
F32 = jnp.float32


def arrived(ref, sem):
    pltpu.make_async_copy(ref, ref, sem).wait()


def selection(n, source):
    out = lax.broadcasted_iota(jnp.int32, (n, n), 0)
    take = lax.broadcasted_iota(jnp.int32, (n, n), 1)
    return (take == source(out)).astype(F32).astype(BF16)


def norm(x, gain):
    scale = lax.rsqrt(jnp.mean(x * x, axis=-1, keepdims=True) + 1e-06)
    return (x * scale * gain).astype(BF16)


def project(x, gain, w_ref, q_ref, kt_ref, v_ref, line, at, n):
    normed = norm(x.astype(F32), gain)
    q = jnp.dot(normed, w_ref[:, :D], preferred_element_type=F32)
    q_ref[line, pl.ds(at, n), :] = (q * SCALE).astype(BF16)
    k = jnp.dot(normed, w_ref[:, D : 2 * D], preferred_element_type=F32)
    kt_ref[line, :, pl.ds(at, n)] = k.T.astype(BF16)
    v = jnp.dot(normed, w_ref[:, 2 * D :], preferred_element_type=F32)
    low = lax.broadcasted_iota(jnp.int32, (n, 128), 1) < 64
    for p in range(PAIRS):
        vp = v[:, 128 * p : 128 * p + 128]
        v_ref[line, p, pl.ds(at, n), :128] = jnp.where(low, vp, 0.0).astype(BF16)
        v_ref[line, p, pl.ds(SEQ + at, n), :128] = jnp.where(low, 0.0, vp).astype(BF16)


def attend(q_ref, kt_ref, v_ref, line, at):
    low = lax.broadcasted_iota(jnp.int32, (QB, 128), 1) < 64
    mixed = []
    for p in range(PAIRS):
        q = q_ref[line, pl.ds(at, QB), 128 * p : 128 * p + 128].astype(F32)
        both = jnp.concatenate([jnp.where(low, q, 0.0), jnp.where(low, 0.0, q)], axis=0).astype(BF16)
        scores = jnp.dot(both, kt_ref[line, 128 * p : 128 * p + 128, :], preferred_element_type=F32)
        weights = jnp.exp2(scores - jnp.max(scores, axis=-1, keepdims=True)).astype(BF16)
        weights = jnp.concatenate([weights[:QB], weights[QB:]], axis=1)
        total = jnp.dot(weights, v_ref[line, p], preferred_element_type=F32)
        mixed.append((total[:, :128] / total[:, 128:]).astype(BF16))
    return jnp.concatenate(mixed, axis=1)


def kernel(
    grid_ref, gain_lon, qkv_lon, out_lon, gain_lat, qkv_lat, out_lat, result_ref,
    w1, o1, w2, o2, x1, x2, q_ref, kt_ref, v_ref, pick, pick3, away, here, done, back, final,
    w_sem, x_sem, x_sent, h_sem, h_sent, b_sem, b_sent, f_sem,
):
    r, c = lax.axis_index("rows"), lax.axis_index("cols")
    loads = [
        pltpu.make_async_copy(src, dst, w_sem.at[n])
        for n, (src, dst) in enumerate([(qkv_lon, w1), (out_lon, o1), (qkv_lat, w2), (out_lat, o2)])
    ]
    for load in loads:
        load.start()

    barrier = pltpu.get_barrier_semaphore()

    @pl.loop(1, COLS)
    def _(k):
        pl.semaphore_signal(barrier, inc=1, device_id=(r, lax.rem(c + k, COLS)), device_id_type=MESH)

    @pl.loop(1, ROWS)
    def _(k):
        pl.semaphore_signal(barrier, inc=1, device_id=(lax.rem(r + k, ROWS), c), device_id_type=MESH)

    pick[0] = selection(128, lambda o: (o % 16 // 2) * 16 + 2 * (o // 16) + o % 2)
    pick[1] = selection(128, lambda o: (o % 16 // 2) * 16 + (o // 32) * 4 + (o % 2) * 2 + o // 16 % 2)
    pick3[...] = selection(256, lambda o: (o % 16) * 16 + o // 16)
    ones = (lax.broadcasted_iota(jnp.int32, (SEQ, 128), 1) < 64).astype(F32)
    for line in range(2):
        for p in range(PAIRS):
            v_ref[line, p, :SEQ, 128:] = ones.astype(BF16)
            v_ref[line, p, SEQ:, 128:] = (1.0 - ones).astype(BF16)

    pl.semaphore_wait(barrier, ROWS + COLS - 2)

    for i in range(2):
        pltpu.make_async_copy(grid_ref.at[2 * c + i], x1.at[i, pl.ds(64 * c, 64)], x_sem.at[i]).start()

        @pl.loop(1, COLS)
        def _(k):
            to = lax.rem(c + k, COLS)
            pltpu.make_async_remote_copy(
                grid_ref.at[2 * to + i], x1.at[i, pl.ds(64 * c, 64)], x_sent.at[i], x_sem.at[i],
                device_id=(r, to), device_id_type=MESH,
            ).start()

    loads[0].wait()
    for i in range(2):
        arrived(x1.at[i], x_sem.at[i])
        project(x1[i], gain_lon[...], w1, q_ref, kt_ref, v_ref, i, 0, SEQ)
    loads[1].wait()

    @pl.loop(0, SEQ // QB)
    def _(step):
        block = lax.rem(step + c // 2, SEQ // QB)
        at = pl.multiple_of(block * QB, QB)
        first = []
        for i in range(2):
            mixed = attend(q_ref, kt_ref, v_ref, i, at)
            total = x1[i, pl.ds(at, QB), :].astype(F32) + jnp.dot(mixed, o1[...], preferred_element_type=F32)
            first.append(total.astype(BF16))
        for g in range(QB // 16):
            cells = jnp.concatenate(
                [first[i][16 * g : 16 * g + 16, 128 * f : 128 * f + 128] for f in range(4) for i in range(2)], axis=0
            )
            cells = jnp.dot(pick[0], cells, preferred_element_type=F32).astype(BF16)
            away[pl.ds(block * (QB // 2) + 8 * g, 8)] = cells.reshape(8, 16, 128)

        @pl.loop(0, ROWS)
        def _(k):
            to_r = lax.rem(r + k, ROWS)
            for n in range(2):
                to_c = 2 * block + n
                own = jnp.logical_and(k == 0, to_c == c)
                src, dst = away.at[to_c * ROWS + to_r], here.at[r * COLS + c]

                @pl.when(own)
                def _():
                    pltpu.make_async_copy(src, dst, h_sem).start()

                @pl.when(jnp.logical_not(own))
                def _():
                    pltpu.make_async_remote_copy(
                        src, dst, h_sent, h_sem, device_id=(to_r, to_c), device_id_type=MESH
                    ).start()

    for load in loads[2:]:
        load.wait()
    arrived(here, h_sem)

    @pl.loop(0, ROWS // 2)
    def _(n):
        pair = [here[pl.ds((2 * n + m) * COLS, COLS)].reshape(128, 128) for m in range(2)]
        cells = jnp.dot(pick[1], jnp.concatenate(pair, axis=1), preferred_element_type=F32).astype(BF16)
        for m in range(2):
            for f in range(4):
                for j in range(2):
                    x2[j, pl.ds((2 * n + m) * 16, 16), 128 * f : 128 * f + 128] = cells[
                        32 * f + 16 * j : 32 * f + 16 * j + 16, 128 * m : 128 * m + 128
                    ]

    for j in range(2):
        project(x2[j], gain_lat[...], w2, q_ref, kt_ref, v_ref, j, 0, SEQ)

        @pl.loop(0, SEQ // QB)
        def _(step):
            block = lax.rem(step + r // 8, SEQ // QB)
            at = pl.multiple_of(block * QB, QB)
            mixed = attend(q_ref, kt_ref, v_ref, j, at)
            total = x2[j, pl.ds(at, QB), :].astype(F32) + jnp.dot(mixed, o2[...], preferred_element_type=F32)
            done[j, pl.ds(at, QB), :] = total.astype(BF16)

            @pl.loop(0, QB // 16)
            def _(k):
                to = block * (QB // 16) + lax.rem(r + k, QB // 16)
                src = done.at[j, pl.ds(pl.multiple_of(to * 16, 16), 16)]
                dst = back.at[2 * r + j]

                @pl.when(to == r)
                def _():
                    pltpu.make_async_copy(src, dst, b_sem.at[r // 8]).start()

                @pl.when(to != r)
                def _():
                    pltpu.make_async_remote_copy(
                        src, dst, b_sent, b_sem.at[r // 8], device_id=(to, c), device_id_type=MESH
                    ).start()

    for g in range(4):
        arrived(back.at[pl.ds(16 * g, 16)], b_sem.at[g])
        cells = back[pl.ds(16 * g, 16)].reshape(256, D)
        cells = jnp.dot(pick3[...], cells, preferred_element_type=F32).astype(BF16)
        final[:, 16 * g : 16 * g + 16, :] = cells.reshape(16, 16, D)
    pltpu.make_async_copy(final, result_ref, f_sem).start()

    for i in range(2):
        arrived(x1.at[i, pl.ds(0, 64 * (COLS - 1))], x_sent.at[i])
    arrived(away.at[pl.ds(0, ROWS * COLS - 1)], h_sent)
    arrived(back.at[pl.ds(0, 2 * (ROWS - 1))], b_sent)
    pltpu.make_async_copy(final, result_ref, f_sem).wait()


def per_device(grid, gain_lon, qkv_lon, out_lon, gain_lat, qkv_lat, out_lat):
    place = pl.BlockSpec(memory_space=pl.ANY)
    whole = pl.BlockSpec(memory_space=pltpu.VMEM)
    dma = pltpu.SemaphoreType.DMA
    return pl.pallas_call(
        kernel,
        out_shape=jax.ShapeDtypeStruct((16, 64, D), BF16),
        in_specs=[place, whole, place, place, whole, place, place],
        out_specs=place,
        scratch_shapes=[
            pltpu.VMEM((D, 3 * D), BF16),
            pltpu.VMEM((D, D), BF16),
            pltpu.VMEM((D, 3 * D), BF16),
            pltpu.VMEM((D, D), BF16),
            pltpu.VMEM((2, SEQ, D), BF16),
            pltpu.VMEM((2, SEQ, D), BF16),
            pltpu.VMEM((2, SEQ, D), BF16),
            pltpu.VMEM((2, D, SEQ), BF16),
            pltpu.VMEM((2, PAIRS, 2 * SEQ, 256), BF16),
            pltpu.VMEM((2, 128, 128), BF16),
            pltpu.VMEM((256, 256), BF16),
            pltpu.VMEM((ROWS * COLS, 16, 128), BF16),
            pltpu.VMEM((ROWS * COLS, 16, 128), BF16),
            pltpu.VMEM((2, SEQ, D), BF16),
            pltpu.VMEM((64, 16, D), BF16),
            pltpu.VMEM((16, 64, D), BF16),
            dma((4,)),
            dma((2,)),
            dma((2,)),
            dma,
            dma,
            dma((4,)),
            dma,
            dma,
        ],
        compiler_params=pltpu.CompilerParams(
            collective_id=0, has_side_effects=True, vmem_limit_bytes=48 * 2**20
        ),
        cost_estimate=pl.CostEstimate(flops=6 * 10**9, bytes_accessed=8 * 2**20, transcendentals=8 * 2**20),
    )(grid, gain_lon.reshape(1, D), qkv_lon, out_lon, gain_lat.reshape(1, D), qkv_lat, out_lat)


def solution(mesh):
    return jax.shard_map(
        per_device,
        mesh=mesh,
        in_specs=(P("rows", "cols", None), P(), P(), P(), P(), P(), P()),
        out_specs=P("rows", "cols", None),
        check_vma=False,
    )
```

```python
import functools

import jax
import jax.numpy as jnp
from jax import lax
from jax.experimental import pallas as pl
from jax.experimental.pallas import tpu as pltpu
from jax.sharding import PartitionSpec as P

D = 512
PAIRS = 4
SEQ = 512
ROWS = 32
COLS = 8
QB = 128
SCALE = 64 ** (-0.5) * 1.4426950408889634
MESH = pl.DeviceIdType.MESH
BF16 = jnp.bfloat16
F32 = jnp.float32


def arrived(ref, sem):
    pltpu.make_async_copy(ref, ref, sem).wait()


def selection(n, source):
    out = lax.broadcasted_iota(jnp.int32, (n, n), 0)
    take = lax.broadcasted_iota(jnp.int32, (n, n), 1)
    return (take == source(out)).astype(F32).astype(BF16)


def norm(x, gain):
    scale = lax.rsqrt(jnp.mean(x * x, axis=-1, keepdims=True) + 1e-06)
    return (x * scale * gain).astype(BF16)


def project(x, gain, w_ref, q_ref, kt_ref, v_ref, line, at, n):
    normed = norm(x.astype(F32), gain)
    q = jnp.dot(normed, w_ref[:, :D], preferred_element_type=F32)
    q_ref[line, pl.ds(at, n), :] = (q * SCALE).astype(BF16)
    k = jnp.dot(normed, w_ref[:, D : 2 * D], preferred_element_type=F32)
    kt_ref[line, :, pl.ds(at, n)] = k.T.astype(BF16)
    v = jnp.dot(normed, w_ref[:, 2 * D :], preferred_element_type=F32)
    low = lax.broadcasted_iota(jnp.int32, (n, 128), 1) < 64
    for p in range(PAIRS):
        vp = v[:, 128 * p : 128 * p + 128]
        v_ref[line, p, pl.ds(at, n), :128] = jnp.where(low, vp, 0.0).astype(BF16)
        v_ref[line, p, pl.ds(SEQ + at, n), :128] = jnp.where(low, 0.0, vp).astype(BF16)


def attend(q_ref, kt_ref, v_ref, line, at):
    low = lax.broadcasted_iota(jnp.int32, (QB, 128), 1) < 64
    mixed = []
    for p in range(PAIRS):
        q = q_ref[line, pl.ds(at, QB), 128 * p : 128 * p + 128].astype(F32)
        both = jnp.concatenate([jnp.where(low, q, 0.0), jnp.where(low, 0.0, q)], axis=0).astype(BF16)
        scores = jnp.dot(both, kt_ref[line, 128 * p : 128 * p + 128, :], preferred_element_type=F32)
        weights = jnp.exp2(scores - jnp.max(scores, axis=-1, keepdims=True)).astype(BF16)
        weights = jnp.concatenate([weights[:QB], weights[QB:]], axis=1)
        total = jnp.dot(weights, v_ref[line, p], preferred_element_type=F32)
        mixed.append((total[:, :128] / total[:, 128:]).astype(BF16))
    return jnp.concatenate(mixed, axis=1)


def kernel(
    grid_ref, gain_lon, qkv_lon, out_lon, gain_lat, qkv_lat, out_lat, result_ref,
    w1, o1, w2, o2, x1, x2, q_ref, kt_ref, v_ref, pick, pick3, away, here, done, back, final,
    w_sem, x_sem, x_sent, go, h_sem, h_sent, b_sem, b_sent, f_sem,
):
    r, c = lax.axis_index("rows"), lax.axis_index("cols")
    core, chip = lax.rem(r, 2), r // 2
    place = core * 16 + chip
    loads = [
        pltpu.make_async_copy(src, dst, w_sem.at[n])
        for n, (src, dst) in enumerate([(qkv_lon, w1), (out_lon, o1), (qkv_lat, w2), (out_lat, o2)])
    ]
    for load in loads:
        load.start()

    barrier = pltpu.get_barrier_semaphore()

    @pl.loop(1, COLS)
    def _(k):
        pl.semaphore_signal(barrier, inc=1, device_id=(r, lax.rem(c + k, COLS)), device_id_type=MESH)

    @pl.loop(1, ROWS)
    def _(k):
        pl.semaphore_signal(barrier, inc=1, device_id=(lax.rem(r + k, ROWS), c), device_id_type=MESH)

    pick[0] = selection(128, lambda o: (o % 16 // 2) * 16 + 2 * (o // 16) + o % 2)
    pick[1] = selection(128, lambda o: (o % 16 // 2) * 16 + (o // 32) * 4 + (o % 2) * 2 + o // 16 % 2)
    pick3[...] = selection(256, lambda o: (o % 16) * 16 + o // 16)
    ones = (lax.broadcasted_iota(jnp.int32, (SEQ, 128), 1) < 64).astype(F32)
    for line in range(2):
        for p in range(PAIRS):
            v_ref[line, p, :SEQ, 128:] = ones.astype(BF16)
            v_ref[line, p, SEQ:, 128:] = (1.0 - ones).astype(BF16)

    pl.semaphore_wait(barrier, ROWS + COLS - 2)

    for i in range(2):
        pltpu.make_async_copy(grid_ref.at[2 * c + i], x1.at[i, :, c], x_sem.at[i]).start()

    @pl.when(core == 1)
    def _():
        pl.semaphore_wait(go, 1)

    for i in range(2):

        @pl.loop(1, COLS)
        def _(k):
            to = lax.rem(c + k, COLS)
            pltpu.make_async_remote_copy(
                grid_ref.at[2 * to + i], x1.at[i, :, c], x_sent.at[i], x_sem.at[i],
                device_id=(r, to), device_id_type=MESH,
            ).start()

    loads[0].wait()
    for i in range(2):
        arrived(x1.at[i], x_sem.at[i])
        if i == 0:

            @pl.when(core == 0)
            def _():
                pl.semaphore_signal(go, inc=1, device_id=(r + 1, c), device_id_type=MESH)

        project(x1[i].reshape(SEQ, D), gain_lon[...], w1, q_ref, kt_ref, v_ref, i, 0, SEQ)
    loads[1].wait()

    @pl.loop(0, SEQ // QB)
    def _(step):
        to_core, part = step // 2, lax.rem(step + chip, 2)
        block = 2 * to_core + part
        at = pl.multiple_of(block * QB, QB)
        first = []
        for i in range(2):
            mixed = attend(q_ref, kt_ref, v_ref, i, at)
            base = x1[i, to_core, pl.ds(4 * part, 4)].reshape(QB, D)
            total = base.astype(F32) + jnp.dot(mixed, o1[...], preferred_element_type=F32)
            first.append(total.astype(BF16))
        for g in range(QB // 16):
            cells = jnp.concatenate(
                [first[i][16 * g : 16 * g + 16, 128 * f : 128 * f + 128] for f in range(4) for i in range(2)], axis=0
            )
            cells = jnp.dot(pick[0], cells, preferred_element_type=F32).astype(BF16)
            away[pl.ds(block * (QB // 2) + 8 * g, 8)] = cells.reshape(8, 16, 128)

        def send(k, n):
            to_chip = lax.rem(chip + k, ROWS // 2)
            turn = lax.rem(c + n, 4)
            to = (2 * to_chip + to_core, 4 * part + turn)
            src, dst = away.at[64 * block + 16 * turn + to_chip], here.at[COLS * place + c]
            return to, src, dst, pltpu.make_async_remote_copy(
                src, dst, h_sent, h_sem.at[core], device_id=to, device_id_type=MESH
            )

        for n in range(4):
            to, src, dst, copy = send(0, n)
            own = jnp.logical_and(to[0] == r, to[1] == c)

            @pl.when(own)
            def _():
                pltpu.make_async_copy(src, dst, h_sem.at[core]).start()

            @pl.when(jnp.logical_not(own))
            def _():
                copy.start()

        @pl.loop(1, ROWS // 2)
        def _(k):
            for n in range(4):
                send(k, n)[-1].start()

    for load in loads[2:]:
        load.wait()

    half = ROWS * COLS // 2
    for h in range(2):
        arrived(here.at[pl.ds(half * h, half)], h_sem.at[h])

        @pl.loop(0, ROWS // 4)
        def _(n):
            first = ROWS // 2 * h + 2 * n
            pair = [here[pl.ds((first + m) * COLS, COLS)].reshape(128, 128) for m in range(2)]
            cells = jnp.dot(pick[1], jnp.concatenate(pair, axis=1), preferred_element_type=F32).astype(BF16)
            for m in range(2):
                for f in range(4):
                    for j in range(2):
                        x2[j, pl.ds((first + m) * 16, 16), 128 * f : 128 * f + 128] = cells[
                            32 * f + 16 * j : 32 * f + 16 * j + 16, 128 * m : 128 * m + 128
                        ]

        for j in range(2):
            n = SEQ // 2
            project(x2[j, n * h : n * h + n], gain_lat[...], w2, q_ref, kt_ref, v_ref, j, n * h, n)

    for j in range(2):

        @pl.loop(0, SEQ // QB)
        def _(step):
            block = lax.rem(step + place // 8, SEQ // QB)
            at = pl.multiple_of(block * QB, QB)
            mixed = attend(q_ref, kt_ref, v_ref, j, at)
            total = x2[j, pl.ds(at, QB), :].astype(F32) + jnp.dot(mixed, o2[...], preferred_element_type=F32)
            done[j, pl.ds(at, QB), :] = total.astype(BF16)

            def send(k):
                to_place = 8 * block + lax.rem(place + k, 8)
                to = 2 * lax.rem(to_place, 16) + to_place // 16
                src, dst = done.at[j, pl.ds(pl.multiple_of(16 * to_place, 16), 16)], back.at[2 * place + j]
                return to, src, dst, pltpu.make_async_remote_copy(
                    src, dst, b_sent, b_sem.at[place // 8], device_id=(to, c), device_id_type=MESH
                )

            to, src, dst, copy = send(0)

            @pl.when(to == r)
            def _():
                pltpu.make_async_copy(src, dst, b_sem.at[place // 8]).start()

            @pl.when(to != r)
            def _():
                copy.start()

            @pl.loop(1, QB // 16)
            def _(k):
                send(k)[-1].start()

    outs = []
    for g in range(4):
        arrived(back.at[pl.ds(16 * g, 16)], b_sem.at[g])
        cells = back[pl.ds(16 * g, 16)].reshape(256, D)
        cells = jnp.dot(pick3[...], cells, preferred_element_type=F32).astype(BF16)
        final[:, 16 * g : 16 * g + 16, :] = cells.reshape(16, 16, D)
        outs.append(
            pltpu.make_async_copy(
                final.at[:, pl.ds(16 * g, 16)], result_ref.at[:, pl.ds(16 * g, 16)], f_sem.at[g]
            )
        )
        outs[-1].start()

    for i in range(2):
        arrived(x1.at[i, :, pl.ds(0, COLS - 1)], x_sent.at[i])
    arrived(away.at[pl.ds(0, ROWS * COLS - 1)], h_sent)
    arrived(back.at[pl.ds(0, 2 * (ROWS - 1))], b_sent)
    for out in outs:
        out.wait()


def per_device(grid, gain_lon, qkv_lon, out_lon, gain_lat, qkv_lat, out_lat):
    place = pl.BlockSpec(memory_space=pl.ANY)
    whole = pl.BlockSpec(memory_space=pltpu.VMEM)
    dma = pltpu.SemaphoreType.DMA
    return pl.pallas_call(
        kernel,
        out_shape=jax.ShapeDtypeStruct((16, 64, D), BF16),
        in_specs=[place, whole, place, place, whole, place, place],
        out_specs=place,
        scratch_shapes=[
            pltpu.VMEM((D, 3 * D), BF16),
            pltpu.VMEM((D, D), BF16),
            pltpu.VMEM((D, 3 * D), BF16),
            pltpu.VMEM((D, D), BF16),
            pltpu.VMEM((2, 2, COLS, 32, D), BF16),
            pltpu.VMEM((2, SEQ, D), BF16),
            pltpu.VMEM((2, SEQ, D), BF16),
            pltpu.VMEM((2, D, SEQ), BF16),
            pltpu.VMEM((2, PAIRS, 2 * SEQ, 256), BF16),
            pltpu.VMEM((2, 128, 128), BF16),
            pltpu.VMEM((256, 256), BF16),
            pltpu.VMEM((ROWS * COLS, 16, 128), BF16),
            pltpu.VMEM((ROWS * COLS, 16, 128), BF16),
            pltpu.VMEM((2, SEQ, D), BF16),
            pltpu.VMEM((64, 16, D), BF16),
            pltpu.VMEM((16, 64, D), BF16),
            dma((4,)),
            dma((2,)),
            dma((2,)),
            pltpu.SemaphoreType.REGULAR,
            dma((2,)),
            dma,
            dma((4,)),
            dma,
            dma((4,)),
        ],
        compiler_params=pltpu.CompilerParams(
            collective_id=0, has_side_effects=True, vmem_limit_bytes=48 * 2**20
        ),
        cost_estimate=pl.CostEstimate(flops=6 * 10**9, bytes_accessed=8 * 2**20, transcendentals=8 * 2**20),
    )(grid.reshape(16, 2, 32, D), gain_lon.reshape(1, D), qkv_lon, out_lon, gain_lat.reshape(1, D), qkv_lat, out_lat)


def solution(mesh):
    return jax.shard_map(
        per_device,
        mesh=mesh,
        in_specs=(P("rows", "cols", None), P(), P(), P(), P(), P(), P()),
        out_specs=P("rows", "cols", None),
        check_vma=False,
    )
```

```python
import functools

import jax
import jax.numpy as jnp
from jax import lax
from jax.experimental import pallas as pl
from jax.experimental.pallas import tpu as pltpu
from jax.sharding import PartitionSpec as P

D = 512
PAIRS = 4
SEQ = 512
ROWS = 32
COLS = 8
QB = 128
SCALE = 64 ** (-0.5) * 1.4426950408889634
MESH = pl.DeviceIdType.MESH
BF16 = jnp.bfloat16
F32 = jnp.float32


def arrived(ref, sem):
    pltpu.make_async_copy(ref, ref, sem).wait()


def selection(n, source):
    out = lax.broadcasted_iota(jnp.int32, (n, n), 0)
    take = lax.broadcasted_iota(jnp.int32, (n, n), 1)
    return (take == source(out)).astype(F32).astype(BF16)


def norm(x, gain):
    scale = lax.rsqrt(jnp.mean(x * x, axis=-1, keepdims=True) + 1e-06)
    return (x * scale * gain).astype(BF16)


def project(x, gain, w_ref, q_ref, kt_ref, v_ref, line, at, n):
    normed = norm(x.astype(F32), gain)
    q = jnp.dot(normed, w_ref[:, :D], preferred_element_type=F32)
    q_ref[line, pl.ds(at, n), :] = (q * SCALE).astype(BF16)
    k = jnp.dot(normed, w_ref[:, D : 2 * D], preferred_element_type=F32)
    kt_ref[line, :, pl.ds(at, n)] = k.T.astype(BF16)
    v = jnp.dot(normed, w_ref[:, 2 * D :], preferred_element_type=F32)
    low = lax.broadcasted_iota(jnp.int32, (n, 128), 1) < 64
    for p in range(PAIRS):
        vp = v[:, 128 * p : 128 * p + 128]
        v_ref[line, p, pl.ds(at, n), :128] = jnp.where(low, vp, 0.0).astype(BF16)
        v_ref[line, p, pl.ds(SEQ + at, n), :128] = jnp.where(low, 0.0, vp).astype(BF16)


def attend(q_ref, kt_ref, v_ref, line, at):
    low = lax.broadcasted_iota(jnp.int32, (QB, 128), 1) < 64
    mixed = []
    for p in range(PAIRS):
        q = q_ref[line, pl.ds(at, QB), 128 * p : 128 * p + 128].astype(F32)
        both = jnp.concatenate([jnp.where(low, q, 0.0), jnp.where(low, 0.0, q)], axis=0).astype(BF16)
        scores = jnp.dot(both, kt_ref[line, 128 * p : 128 * p + 128, :], preferred_element_type=F32)
        weights = jnp.exp2(scores - jnp.max(scores, axis=-1, keepdims=True)).astype(BF16)
        weights = jnp.concatenate([weights[:QB], weights[QB:]], axis=1)
        total = jnp.dot(weights, v_ref[line, p], preferred_element_type=F32)
        mixed.append((total[:, :128] / total[:, 128:]).astype(BF16))
    return jnp.concatenate(mixed, axis=1)


def kernel(
    grid_ref, gain_lon, qkv_lon, out_lon, gain_lat, qkv_lat, out_lat, result_ref,
    g1, w1, o1, g2, w2, o2, x1, x2, q_ref, kt_ref, v_ref, pick, pick3, away, here, done, back, final,
    w_sem, x_sem, x_sent, go, met, known, h_sem, h_sent, b_sem, b_sent, f_sem,
):
    r, c = lax.axis_index("rows"), lax.axis_index("cols")
    core, chip = lax.rem(r, 2), r // 2
    place = core * 16 + chip
    loads = [
        pltpu.make_async_copy(src, dst, w_sem.at[n])
        for n, (src, dst) in enumerate(
            [(gain_lon, g1), (qkv_lon, w1), (out_lon, o1), (gain_lat, g2), (qkv_lat, w2), (out_lat, o2)]
        )
    ]
    for load in loads:
        load.start()

    barrier = pltpu.get_barrier_semaphore()

    @pl.loop(1, COLS)
    def _(k):
        pl.semaphore_signal(barrier, inc=1, device_id=(r, lax.rem(c + k, COLS)), device_id_type=MESH)

    four = [r + (1 - 2 * core), lax.rem(r + 16, ROWS), lax.rem(r + 16, ROWS) + (1 - 2 * core)]

    @pl.loop(1, 8)
    def _(k):
        to = r // 16 * 16 + lax.rem(r + 2 * k, 16)
        pl.semaphore_signal(barrier, inc=1, device_id=(to, c), device_id_type=MESH)

    for to in four:
        pl.semaphore_signal(barrier, inc=1, device_id=(to, c), device_id_type=MESH)

    pick[0] = selection(128, lambda o: (o % 8 // 2) * 32 + 2 * (o // 8) + o % 2)
    pick[1] = selection(128, lambda o: (o % 2) * 64 + (o % 16 // 2) * 8 + (o // 32) * 2 + o // 16 % 2)
    pick3[...] = selection(256, lambda o: (o % 16) * 16 + o // 16)
    ones = (lax.broadcasted_iota(jnp.int32, (SEQ, 128), 1) < 64).astype(F32)
    for line in range(2):
        for p in range(PAIRS):
            v_ref[line, p, :SEQ, 128:] = ones.astype(BF16)
            v_ref[line, p, SEQ:, 128:] = (1.0 - ones).astype(BF16)

    pl.semaphore_wait(barrier, 17)
    for to in four:
        pl.semaphore_signal(met, inc=1, device_id=(to, c), device_id_type=MESH)

    for i in range(2):
        pltpu.make_async_copy(grid_ref.at[2 * c + i], x1.at[i, :, c], x_sem.at[i]).start()

    @pl.when(core == 1)
    def _():
        pl.semaphore_wait(go, 1)

    for i in range(2):

        @pl.loop(1, COLS)
        def _(k):
            to = lax.rem(c + k, COLS)
            pltpu.make_async_remote_copy(
                grid_ref.at[2 * to + i], x1.at[i, :, c], x_sent.at[i], x_sem.at[i],
                device_id=(r, to), device_id_type=MESH,
            ).start()

    def row_block(i, to_core, part):
        block = 2 * to_core + part
        at = pl.multiple_of(block * QB, QB)
        mixed = attend(q_ref, kt_ref, v_ref, i, at)
        base = x1[i, to_core, pl.ds(4 * part, 4)].reshape(QB, D)
        first = base.astype(F32) + jnp.dot(mixed, o1[...], preferred_element_type=F32)
        first = first.astype(BF16)
        for g in range(QB // 32):
            cells = jnp.concatenate(
                [first[32 * g : 32 * g + 32, 128 * f : 128 * f + 128] for f in range(4)], axis=0
            )
            cells = jnp.dot(pick[0], cells, preferred_element_type=F32)
            away[i, pl.ds(block * (QB // 2) + 16 * g, 16)] = cells.reshape(16, 8, 128).astype(BF16)

        def send(k, n):
            to_chip = lax.rem(chip + k, ROWS // 2)
            turn = lax.rem(c + n, 4)
            to = (2 * to_chip + to_core, 4 * part + turn)
            src, dst = away.at[i, 64 * block + 16 * turn + to_chip], here.at[core, i, COLS * chip + c]
            return to, src, dst, pltpu.make_async_remote_copy(
                src, dst, h_sent, h_sem.at[core], device_id=to, device_id_type=MESH
            )

        for n in range(4):
            to, src, dst, copy = send(0, n)
            own = jnp.logical_and(to[0] == r, to[1] == c)

            @pl.when(own)
            def _():
                pltpu.make_async_copy(src, dst, h_sem.at[core]).start()

            @pl.when(jnp.logical_not(own))
            def _():
                copy.start()

        @pl.loop(1, ROWS // 2)
        def _(k):
            for n in range(4):
                send(k, n)[-1].start()

    pl.semaphore_wait(met, 3)

    @pl.loop(1, COLS)
    def _(k):
        pl.semaphore_signal(known, inc=1, device_id=(r, lax.rem(c + k, COLS)), device_id_type=MESH)

    loads[0].wait()
    loads[1].wait()
    for i in range(2):
        arrived(x1.at[i], x_sem.at[i])
        if i == 0:

            @pl.when(core == 0)
            def _():
                pl.semaphore_signal(go, inc=1, device_id=(r + 1, c), device_id_type=MESH)

        project(x1[i].reshape(SEQ, D), g1[...], w1, q_ref, kt_ref, v_ref, i, 0, SEQ)
        if i == 0:
            loads[2].wait()
            pl.semaphore_wait(known, COLS - 1)

            @pl.loop(0, 2)
            def _(step):
                row_block(0, 0, lax.rem(step + chip, 2))

    @pl.loop(0, 6)
    def _(step):
        turn = step // 2 + 1
        row_block(lax.rem(turn, 2), turn // 2, lax.rem(step + chip, 2))

    for load in loads[3:]:
        load.wait()

    for h in range(2):
        arrived(here.at[h], h_sem.at[h])

        @pl.loop(0, ROWS // 4)
        def _(n):
            first = ROWS // 2 * h + 2 * n
            pair = [
                jnp.concatenate(
                    [
                        here[h, i, pl.ds((2 * n + m) * COLS, COLS)].astype(F32).reshape(64, 128).astype(BF16)
                        for i in range(2)
                    ],
                    axis=0,
                )
                for m in range(2)
            ]
            cells = jnp.dot(pick[1], jnp.concatenate(pair, axis=1), preferred_element_type=F32).astype(BF16)
            for m in range(2):
                for f in range(4):
                    for j in range(2):
                        x2[j, pl.ds((first + m) * 16, 16), 128 * f : 128 * f + 128] = cells[
                            32 * f + 16 * j : 32 * f + 16 * j + 16, 128 * m : 128 * m + 128
                        ]

        for j in range(2):
            n = SEQ // 2
            project(x2[j, n * h : n * h + n], g2[...], w2, q_ref, kt_ref, v_ref, j, n * h, n)

    for j in range(2):

        @pl.loop(0, SEQ // QB)
        def _(step):
            block = lax.rem(step + place // 8, SEQ // QB)
            at = pl.multiple_of(block * QB, QB)
            mixed = attend(q_ref, kt_ref, v_ref, j, at)
            total = x2[j, pl.ds(at, QB), :].astype(F32) + jnp.dot(mixed, o2[...], preferred_element_type=F32)
            done[j, pl.ds(at, QB), :] = total.astype(BF16)

            def send(k):
                to_place = 8 * block + lax.rem(place + k, 8)
                to = 2 * lax.rem(to_place, 16) + to_place // 16
                src, dst = done.at[j, pl.ds(pl.multiple_of(16 * to_place, 16), 16)], back.at[2 * place + j]
                return to, src, dst, pltpu.make_async_remote_copy(
                    src, dst, b_sent, b_sem.at[place // 8], device_id=(to, c), device_id_type=MESH
                )

            to, src, dst, copy = send(0)

            @pl.when(to == r)
            def _():
                pltpu.make_async_copy(src, dst, b_sem.at[place // 8]).start()

            @pl.when(to != r)
            def _():
                copy.start()

            @pl.loop(1, QB // 16)
            def _(k):
                send(k)[-1].start()

    outs = []
    for g in range(4):
        arrived(back.at[pl.ds(16 * g, 16)], b_sem.at[g])
        cells = back[pl.ds(16 * g, 16)].reshape(256, D)
        cells = jnp.dot(pick3[...], cells, preferred_element_type=F32).astype(BF16)
        final[:, 16 * g : 16 * g + 16, :] = cells.reshape(16, 16, D)
        outs.append(
            pltpu.make_async_copy(
                final.at[:, pl.ds(16 * g, 16)], result_ref.at[:, pl.ds(16 * g, 16)], f_sem.at[g]
            )
        )
        outs[-1].start()

    for i in range(2):
        arrived(x1.at[i, :, pl.ds(0, COLS - 1)], x_sent.at[i])
    arrived(away.at[:, pl.ds(0, ROWS * COLS - 1)], h_sent)
    arrived(back.at[pl.ds(0, 2 * (ROWS - 1))], b_sent)
    for out in outs:
        out.wait()


def per_device(grid, gain_lon, qkv_lon, out_lon, gain_lat, qkv_lat, out_lat):
    place = pl.BlockSpec(memory_space=pltpu.HBM)
    dma = pltpu.SemaphoreType.DMA
    return pl.pallas_call(
        kernel,
        out_shape=jax.ShapeDtypeStruct((16, 64, D), BF16),
        in_specs=[place] * 7,
        out_specs=pl.BlockSpec(memory_space=pl.ANY),
        scratch_shapes=[
            pltpu.VMEM((1, D), F32),
            pltpu.VMEM((D, 3 * D), BF16),
            pltpu.VMEM((D, D), BF16),
            pltpu.VMEM((1, D), F32),
            pltpu.VMEM((D, 3 * D), BF16),
            pltpu.VMEM((D, D), BF16),
            pltpu.VMEM((2, 2, COLS, 32, D), BF16),
            pltpu.VMEM((2, SEQ, D), BF16),
            pltpu.VMEM((2, SEQ, D), BF16),
            pltpu.VMEM((2, D, SEQ), BF16),
            pltpu.VMEM((2, PAIRS, 2 * SEQ, 256), BF16),
            pltpu.VMEM((2, 128, 128), BF16),
            pltpu.VMEM((256, 256), BF16),
            pltpu.VMEM((2, ROWS * COLS, 8, 128), BF16),
            pltpu.VMEM((2, 2, ROWS * COLS // 2, 8, 128), BF16),
            pltpu.VMEM((2, SEQ, D), BF16),
            pltpu.VMEM((64, 16, D), BF16),
            pltpu.VMEM((16, 64, D), BF16),
            dma((6,)),
            dma((2,)),
            dma((2,)),
            pltpu.SemaphoreType.REGULAR,
            pltpu.SemaphoreType.REGULAR,
            pltpu.SemaphoreType.REGULAR,
            dma((2,)),
            dma,
            dma((4,)),
            dma,
            dma((4,)),
        ],
        compiler_params=pltpu.CompilerParams(
            collective_id=0, has_side_effects=True, vmem_limit_bytes=56 * 2**20
        ),
        cost_estimate=pl.CostEstimate(flops=6 * 10**9, bytes_accessed=8 * 2**20, transcendentals=8 * 2**20),
    )(grid.reshape(16, 2, 32, D), gain_lon.reshape(1, D), qkv_lon, out_lon, gain_lat.reshape(1, D), qkv_lat, out_lat)


def solution(mesh):
    return jax.shard_map(
        per_device,
        mesh=mesh,
        in_specs=(P("rows", "cols", None), P(), P(), P(), P(), P(), P()),
        out_specs=P("rows", "cols", None),
        check_vma=False,
    )
```

```python
import functools

import jax
import jax.numpy as jnp
from jax import lax
from jax.experimental import pallas as pl
from jax.experimental.pallas import tpu as pltpu
from jax.sharding import PartitionSpec as P

D = 512
PAIRS = 4
SEQ = 512
ROWS = 32
COLS = 8
QB = 128
SCALE = 64 ** (-0.5) * 1.4426950408889634
MESH = pl.DeviceIdType.MESH
BF16 = jnp.bfloat16
F32 = jnp.float32


def arrived(ref, sem):
    pltpu.make_async_copy(ref, ref, sem).wait()


def selection(n, source):
    out = lax.broadcasted_iota(jnp.int32, (n, n), 0)
    take = lax.broadcasted_iota(jnp.int32, (n, n), 1)
    return (take == source(out)).astype(F32).astype(BF16)


def norm(x, gain):
    scale = lax.rsqrt(jnp.mean(x * x, axis=-1, keepdims=True) + 1e-06)
    return (x * scale * gain).astype(BF16)


def project(x, gain, w_ref, q_ref, kt_ref, v_ref, line, at, n):
    normed = norm(x.astype(F32), gain)
    q = jnp.dot(normed, w_ref[:, :D], preferred_element_type=F32)
    q_ref[line, pl.ds(at, n), :] = (q * SCALE).astype(BF16)
    k = jnp.dot(normed, w_ref[:, D : 2 * D], preferred_element_type=F32)
    kt_ref[line, :, pl.ds(at, n)] = k.T.astype(BF16)
    v = jnp.dot(normed, w_ref[:, 2 * D :], preferred_element_type=F32)
    low = lax.broadcasted_iota(jnp.int32, (n, 128), 1) < 64
    for p in range(PAIRS):
        vp = v[:, 128 * p : 128 * p + 128]
        v_ref[line, p, pl.ds(at, n), :128] = jnp.where(low, vp, 0.0).astype(BF16)
        v_ref[line, p, pl.ds(SEQ + at, n), :128] = jnp.where(low, 0.0, vp).astype(BF16)


def attend(q_ref, kt_ref, v_ref, line, at):
    low = lax.broadcasted_iota(jnp.int32, (QB, 128), 1) < 64
    mixed = []
    for p in range(PAIRS):
        q = q_ref[line, pl.ds(at, QB), 128 * p : 128 * p + 128].astype(F32)
        both = jnp.concatenate([jnp.where(low, q, 0.0), jnp.where(low, 0.0, q)], axis=0).astype(BF16)
        scores = jnp.dot(both, kt_ref[line, 128 * p : 128 * p + 128, :], preferred_element_type=F32)
        weights = jnp.exp2(scores - jnp.max(scores, axis=-1, keepdims=True)).astype(BF16)
        weights = jnp.concatenate([weights[:QB], weights[QB:]], axis=1)
        total = jnp.dot(weights, v_ref[line, p], preferred_element_type=F32)
        mixed.append((total[:, :128] / total[:, 128:]).astype(BF16))
    return jnp.concatenate(mixed, axis=1)


def kernel(
    grid_ref, gain_lon, qkv_lon, out_lon, gain_lat, qkv_lat, out_lat, result_ref,
    g1, w1, o1, g2, w2, o2, x1, x2, q_ref, kt_ref, v_ref, pick, pick3, away, here, done, back, final,
    w_sem, x_sem, x_sent, met, known, h_sem, h_sent, b_sem, b_sent, f_sem,
):
    r, c = lax.axis_index("rows"), lax.axis_index("cols")
    core, chip = lax.rem(r, 2), r // 2
    place = core * 16 + chip
    loads = [
        pltpu.make_async_copy(src, dst, w_sem.at[n])
        for n, (src, dst) in enumerate(
            [(gain_lon, g1), (qkv_lon, w1), (out_lon, o1), (gain_lat, g2), (qkv_lat, w2), (out_lat, o2)]
        )
    ]
    for load in loads:
        load.start()

    barrier = pltpu.get_barrier_semaphore()

    @pl.loop(1, COLS)
    def _(k):
        pl.semaphore_signal(barrier, inc=1, device_id=(r, lax.rem(c + k, COLS)), device_id_type=MESH)

    four = [r + (1 - 2 * core), lax.rem(r + 16, ROWS), lax.rem(r + 16, ROWS) + (1 - 2 * core)]

    @pl.loop(1, 8)
    def _(k):
        to = r // 16 * 16 + lax.rem(r + 2 * k, 16)
        pl.semaphore_signal(barrier, inc=1, device_id=(to, c), device_id_type=MESH)

    for to in four:
        pl.semaphore_signal(barrier, inc=1, device_id=(to, c), device_id_type=MESH)

    pick[0] = selection(128, lambda o: (o % 8 // 2) * 32 + 2 * (o // 8) + o % 2)
    pick[1] = selection(128, lambda o: (o % 2) * 64 + (o % 16 // 2) * 8 + (o // 32) * 2 + o // 16 % 2)
    pick3[...] = selection(256, lambda o: (o % 16) * 16 + o // 16)
    ones = (lax.broadcasted_iota(jnp.int32, (SEQ, 128), 1) < 64).astype(F32)
    for line in range(2):
        for p in range(PAIRS):
            v_ref[line, p, :SEQ, 128:] = ones.astype(BF16)
            v_ref[line, p, SEQ:, 128:] = (1.0 - ones).astype(BF16)

    pl.semaphore_wait(barrier, 17)
    for to in four:
        pl.semaphore_signal(met, inc=1, device_id=(to, c), device_id_type=MESH)

    for i in range(2):
        pltpu.make_async_copy(grid_ref.at[2 * c + i], x1.at[i, :, c], x_sem.at[i]).start()

    def piece(i, h, q, k):
        to, cells = lax.rem(c + k, COLS), pl.ds(16 * q, 16)
        pltpu.make_async_remote_copy(
            grid_ref.at[2 * to + i, h, cells], x1.at[i, h, c, cells], x_sent.at[i], x_sem.at[i],
            device_id=(r, to), device_id_type=MESH,
        ).start()

    for i, h in ((0, 0), (0, 1), (1, 0), (1, 1)):
        for q in range(2):
            for k in (1, 7, 2, 6, 3, 5, 4):
                piece(i, h, q, k)

    def row_block(i, to_core, part):
        block = 2 * to_core + part
        at = pl.multiple_of(block * QB, QB)
        mixed = attend(q_ref, kt_ref, v_ref, i, at)
        base = x1[i, to_core, pl.ds(4 * part, 4)].reshape(QB, D)
        first = base.astype(F32) + jnp.dot(mixed, o1[...], preferred_element_type=F32)
        first = first.astype(BF16)
        for g in range(QB // 32):
            cells = jnp.concatenate(
                [first[32 * g : 32 * g + 32, 128 * f : 128 * f + 128] for f in range(4)], axis=0
            )
            cells = jnp.dot(pick[0], cells, preferred_element_type=F32)
            away[i, pl.ds(block * (QB // 2) + 16 * g, 16)] = cells.reshape(16, 8, 128).astype(BF16)

        def send(k, n):
            to_chip = lax.rem(chip + k, ROWS // 2)
            turn = lax.rem(c + n, 4)
            to = (2 * to_chip + to_core, 4 * part + turn)
            src, dst = away.at[i, 64 * block + 16 * turn + to_chip], here.at[core, i, COLS * chip + c]
            return to, src, dst, pltpu.make_async_remote_copy(
                src, dst, h_sent, h_sem.at[core], device_id=to, device_id_type=MESH
            )

        for n in range(4):
            to, src, dst, copy = send(0, n)
            own = jnp.logical_and(to[0] == r, to[1] == c)

            @pl.when(own)
            def _():
                pltpu.make_async_copy(src, dst, h_sem.at[core]).start()

            @pl.when(jnp.logical_not(own))
            def _():
                copy.start()

        @pl.loop(1, 8)
        def _(k):
            for n in range(4):
                send(k, n)[-1].start()
            for n in range(4):
                send(16 - k, n)[-1].start()

        for n in range(4):
            send(8, n)[-1].start()

    pl.semaphore_wait(met, 3)

    @pl.loop(1, COLS)
    def _(k):
        pl.semaphore_signal(known, inc=1, device_id=(r, lax.rem(c + k, COLS)), device_id_type=MESH)

    loads[0].wait()
    loads[1].wait()
    for i in range(2):
        arrived(x1.at[i], x_sem.at[i])
        project(x1[i].reshape(SEQ, D), g1[...], w1, q_ref, kt_ref, v_ref, i, 0, SEQ)
        if i == 0:
            loads[2].wait()
            pl.semaphore_wait(known, COLS - 1)

            @pl.loop(0, 2)
            def _(step):
                row_block(0, 0, lax.rem(step + chip, 2))

    @pl.loop(0, 6)
    def _(step):
        turn = step // 2 + 1
        row_block(lax.rem(turn, 2), turn // 2, lax.rem(step + chip, 2))

    for load in loads[3:]:
        load.wait()

    for h in range(2):
        arrived(here.at[h], h_sem.at[h])

        @pl.loop(0, ROWS // 4)
        def _(n):
            first = ROWS // 2 * h + 2 * n
            pair = [
                jnp.concatenate(
                    [
                        here[h, i, pl.ds((2 * n + m) * COLS, COLS)].astype(F32).reshape(64, 128).astype(BF16)
                        for i in range(2)
                    ],
                    axis=0,
                )
                for m in range(2)
            ]
            cells = jnp.dot(pick[1], jnp.concatenate(pair, axis=1), preferred_element_type=F32).astype(BF16)
            for m in range(2):
                for f in range(4):
                    for j in range(2):
                        x2[j, pl.ds((first + m) * 16, 16), 128 * f : 128 * f + 128] = cells[
                            32 * f + 16 * j : 32 * f + 16 * j + 16, 128 * m : 128 * m + 128
                        ]

        for j in range(2 - h):
            n = SEQ // 2
            project(x2[j, n * h : n * h + n], g2[...], w2, q_ref, kt_ref, v_ref, j, n * h, n)

    for j in range(2):
        if j == 1:
            n = SEQ // 2
            project(x2[j, n:], g2[...], w2, q_ref, kt_ref, v_ref, j, n, n)

        @pl.loop(0, SEQ // QB)
        def _(step):
            block = lax.rem(step + place // 8, SEQ // QB)
            at = pl.multiple_of(block * QB, QB)
            mixed = attend(q_ref, kt_ref, v_ref, j, at)
            total = x2[j, pl.ds(at, QB), :].astype(F32) + jnp.dot(mixed, o2[...], preferred_element_type=F32)
            done[j, pl.ds(at, QB), :] = total.astype(BF16)

            def send(k):
                to_place = 8 * block + lax.rem(place + k, 8)
                to = 2 * lax.rem(to_place, 16) + to_place // 16
                src, dst = done.at[j, pl.ds(pl.multiple_of(16 * to_place, 16), 16)], back.at[2 * place + j]
                return to, src, dst, pltpu.make_async_remote_copy(
                    src, dst, b_sent, b_sem.at[place // 8], device_id=(to, c), device_id_type=MESH
                )

            to, src, dst, copy = send(0)

            @pl.when(to == r)
            def _():
                pltpu.make_async_copy(src, dst, b_sem.at[place // 8]).start()

            @pl.when(to != r)
            def _():
                copy.start()

            for k in (1, 7, 2, 6, 3, 5, 4):
                send(k)[-1].start()

    outs = []
    for g in range(4):
        arrived(back.at[pl.ds(16 * g, 16)], b_sem.at[g])
        cells = back[pl.ds(16 * g, 16)].reshape(256, D)
        cells = jnp.dot(pick3[...], cells, preferred_element_type=F32).astype(BF16)
        final[:, 16 * g : 16 * g + 16, :] = cells.reshape(16, 16, D)
        outs.append(
            pltpu.make_async_copy(
                final.at[:, pl.ds(16 * g, 16)], result_ref.at[:, pl.ds(16 * g, 16)], f_sem.at[g]
            )
        )
        outs[-1].start()

    for i in range(2):
        arrived(x1.at[i, :, pl.ds(0, COLS - 1)], x_sent.at[i])
    arrived(away.at[:, pl.ds(0, ROWS * COLS - 1)], h_sent)
    arrived(back.at[pl.ds(0, 2 * (ROWS - 1))], b_sent)
    for out in outs:
        out.wait()


def per_device(grid, gain_lon, qkv_lon, out_lon, gain_lat, qkv_lat, out_lat):
    place = pl.BlockSpec(memory_space=pltpu.HBM)
    dma = pltpu.SemaphoreType.DMA
    return pl.pallas_call(
        kernel,
        out_shape=jax.ShapeDtypeStruct((16, 64, D), BF16),
        in_specs=[place] * 7,
        out_specs=pl.BlockSpec(memory_space=pl.ANY),
        scratch_shapes=[
            pltpu.VMEM((1, D), F32),
            pltpu.VMEM((D, 3 * D), BF16),
            pltpu.VMEM((D, D), BF16),
            pltpu.VMEM((1, D), F32),
            pltpu.VMEM((D, 3 * D), BF16),
            pltpu.VMEM((D, D), BF16),
            pltpu.VMEM((2, 2, COLS, 32, D), BF16),
            pltpu.VMEM((2, SEQ, D), BF16),
            pltpu.VMEM((2, SEQ, D), BF16),
            pltpu.VMEM((2, D, SEQ), BF16),
            pltpu.VMEM((2, PAIRS, 2 * SEQ, 256), BF16),
            pltpu.VMEM((2, 128, 128), BF16),
            pltpu.VMEM((256, 256), BF16),
            pltpu.VMEM((2, ROWS * COLS, 8, 128), BF16),
            pltpu.VMEM((2, 2, ROWS * COLS // 2, 8, 128), BF16),
            pltpu.VMEM((2, SEQ, D), BF16),
            pltpu.VMEM((64, 16, D), BF16),
            pltpu.VMEM((16, 64, D), BF16),
            dma((6,)),
            dma((2,)),
            dma((2,)),
            pltpu.SemaphoreType.REGULAR,
            pltpu.SemaphoreType.REGULAR,
            dma((2,)),
            dma,
            dma((4,)),
            dma,
            dma((4,)),
        ],
        compiler_params=pltpu.CompilerParams(
            collective_id=0, has_side_effects=True, vmem_limit_bytes=56 * 2**20
        ),
        cost_estimate=pl.CostEstimate(flops=6 * 10**9, bytes_accessed=8 * 2**20, transcendentals=8 * 2**20),
    )(grid.reshape(16, 2, 32, D), gain_lon.reshape(1, D), qkv_lon, out_lon, gain_lat.reshape(1, D), qkv_lat, out_lat)


def solution(mesh):
    return jax.shard_map(
        per_device,
        mesh=mesh,
        in_specs=(P("rows", "cols", None), P(), P(), P(), P(), P(), P()),
        out_specs=P("rows", "cols", None),
        check_vma=False,
    )
```

```python
import functools

import jax
import jax.numpy as jnp
from jax import lax
from jax.experimental import pallas as pl
from jax.experimental.pallas import tpu as pltpu
from jax.sharding import PartitionSpec as P

D = 512
PAIRS = 4
SEQ = 512
ROWS = 32
COLS = 8
QB = 128
SCALE = 64 ** (-0.5) * 1.4426950408889634
MESH = pl.DeviceIdType.MESH
BF16 = jnp.bfloat16
F32 = jnp.float32


def arrived(ref, sem):
    pltpu.make_async_copy(ref, ref, sem).wait()


def selection(n, source):
    out = lax.broadcasted_iota(jnp.int32, (n, n), 0)
    take = lax.broadcasted_iota(jnp.int32, (n, n), 1)
    return (take == source(out)).astype(F32).astype(BF16)


def norm(x, gain):
    scale = lax.rsqrt(jnp.mean(x * x, axis=-1, keepdims=True) + 1e-06)
    return (x * scale * gain).astype(BF16)


def project(x, gain, w_ref, q_ref, kt_ref, v_ref, line, at, n):
    normed = norm(x.astype(F32), gain)
    q = jnp.dot(normed, w_ref[:, :D], preferred_element_type=F32)
    q_ref[line, pl.ds(at, n), :] = (q * SCALE).astype(BF16)
    k = jnp.dot(normed, w_ref[:, D : 2 * D], preferred_element_type=F32)
    kt_ref[line, :, pl.ds(at, n)] = k.T.astype(BF16)
    v = jnp.dot(normed, w_ref[:, 2 * D :], preferred_element_type=F32)
    low = lax.broadcasted_iota(jnp.int32, (n, 128), 1) < 64
    for p in range(PAIRS):
        vp = v[:, 128 * p : 128 * p + 128]
        v_ref[line, p, pl.ds(at, n), :128] = jnp.where(low, vp, 0.0).astype(BF16)
        v_ref[line, p, pl.ds(SEQ + at, n), :128] = jnp.where(low, 0.0, vp).astype(BF16)


def attend(q_ref, kt_ref, v_ref, line, at):
    low = lax.broadcasted_iota(jnp.int32, (QB, 128), 1) < 64
    mixed = []
    for p in range(PAIRS):
        q = q_ref[line, pl.ds(at, QB), 128 * p : 128 * p + 128].astype(F32)
        both = jnp.concatenate([jnp.where(low, q, 0.0), jnp.where(low, 0.0, q)], axis=0).astype(BF16)
        scores = jnp.dot(both, kt_ref[line, 128 * p : 128 * p + 128, :], preferred_element_type=F32)
        weights = jnp.exp2(scores - jnp.max(scores, axis=-1, keepdims=True)).astype(BF16)
        weights = jnp.concatenate([weights[:QB], weights[QB:]], axis=1)
        total = jnp.dot(weights, v_ref[line, p], preferred_element_type=F32)
        mixed.append((total[:, :128] / total[:, 128:]).astype(BF16))
    return jnp.concatenate(mixed, axis=1)


def kernel(
    grid_ref, gain_lon, qkv_lon, out_lon, gain_lat, qkv_lat, out_lat, result_ref,
    g1, w1, o1, g2, w2, o2, x1, x2, q_ref, kt_ref, v_ref, pick, pick3, away, here, done, back, final,
    w_sem, x_sem, x_sent, met, known, h_sem, h_sent, b_sem, b_sent, f_sem,
):
    r, c = lax.axis_index("rows"), lax.axis_index("cols")
    core, chip = lax.rem(r, 2), r // 2
    place = core * 16 + chip
    loads = [
        pltpu.make_async_copy(src, dst, w_sem.at[n])
        for n, (src, dst) in enumerate(
            [(gain_lon, g1), (qkv_lon, w1), (out_lon, o1), (gain_lat, g2), (qkv_lat, w2), (out_lat, o2)]
        )
    ]
    for load in loads:
        load.start()

    barrier = pltpu.get_barrier_semaphore()

    @pl.loop(1, COLS)
    def _(k):
        pl.semaphore_signal(barrier, inc=1, device_id=(r, lax.rem(c + k, COLS)), device_id_type=MESH)

    four = [r + (1 - 2 * core), lax.rem(r + 16, ROWS), lax.rem(r + 16, ROWS) + (1 - 2 * core)]

    @pl.loop(1, 8)
    def _(k):
        to = r // 16 * 16 + lax.rem(r + 2 * k, 16)
        pl.semaphore_signal(barrier, inc=1, device_id=(to, c), device_id_type=MESH)

    for to in four:
        pl.semaphore_signal(barrier, inc=1, device_id=(to, c), device_id_type=MESH)

    pick[0] = selection(128, lambda o: (o % 8 // 2) * 32 + 2 * (o // 8) + o % 2)
    pick[1] = selection(128, lambda o: (o % 2) * 64 + (o % 16 // 2) * 8 + (o // 32) * 2 + o // 16 % 2)
    pick3[...] = selection(256, lambda o: (o % 16) * 16 + o // 16)
    ones = (lax.broadcasted_iota(jnp.int32, (SEQ, 128), 1) < 64).astype(F32)
    for line in range(2):
        for p in range(PAIRS):
            v_ref[line, p, :SEQ, 128:] = ones.astype(BF16)
            v_ref[line, p, SEQ:, 128:] = (1.0 - ones).astype(BF16)

    pl.semaphore_wait(barrier, 17)
    for to in four:
        pl.semaphore_signal(met, inc=1, device_id=(to, c), device_id_type=MESH)

    for i in range(2):
        for h in range(2):
            pltpu.make_async_copy(grid_ref.at[2 * c + i, h], x1.at[i, h, c], x_sem.at[2 * i + h]).start()

    def piece(i, h, q, k):
        to, cells = lax.rem(c + k, COLS), pl.ds(16 * q, 16)
        pltpu.make_async_remote_copy(
            grid_ref.at[2 * to + i, h, cells], x1.at[i, h, c, cells], x_sent.at[i], x_sem.at[2 * i + h],
            device_id=(r, to), device_id_type=MESH,
        ).start()

    for i, h in ((0, 0), (0, 1), (1, 0), (1, 1)):
        for q in range(2):
            for k in (1, 7, 2, 6, 3, 5, 4):
                piece(i, h, q, k)

    def row_block(i, to_core, part):
        block = 2 * to_core + part
        at = pl.multiple_of(block * QB, QB)
        mixed = attend(q_ref, kt_ref, v_ref, i, at)
        base = x1[i, to_core, pl.ds(4 * part, 4)].reshape(QB, D)
        first = base.astype(F32) + jnp.dot(mixed, o1[...], preferred_element_type=F32)
        first = first.astype(BF16)
        for g in range(QB // 32):
            cells = jnp.concatenate(
                [first[32 * g : 32 * g + 32, 128 * f : 128 * f + 128] for f in range(4)], axis=0
            )
            cells = jnp.dot(pick[0], cells, preferred_element_type=F32)
            away[pl.ds(block * (QB // 2) + 16 * g, 16), i] = cells.reshape(16, 8, 128).astype(BF16)

    def send_block(to_core, part, i):
        block = 2 * to_core + part

        def send(k, n):
            to_chip = lax.rem(chip + k, ROWS // 2)
            turn = lax.rem(c + n, 4)
            to = (2 * to_chip + to_core, 4 * part + turn)
            src, dst = away.at[64 * block + 16 * turn + to_chip], here.at[core, COLS * chip + c]
            if i is not None:
                src, dst = src.at[i], dst.at[i]
            return to, src, dst, pltpu.make_async_remote_copy(
                src, dst, h_sent, h_sem.at[core], device_id=to, device_id_type=MESH
            )

        @pl.loop(0, 4)
        def _(n):
            for k in (4, 12, 3, 13, 5, 11, 2, 14, 6, 10, 1, 15, 7, 9, 8):
                send(k, n)[-1].start()
            to, src, dst, copy = send(0, n)
            own = jnp.logical_and(to[0] == r, to[1] == c)

            @pl.when(own)
            def _():
                pltpu.make_async_copy(src, dst, h_sem.at[core]).start()

            @pl.when(jnp.logical_not(own))
            def _():
                copy.start()

    pl.semaphore_wait(met, 3)

    @pl.loop(1, COLS)
    def _(k):
        pl.semaphore_signal(known, inc=1, device_id=(r, lax.rem(c + k, COLS)), device_id_type=MESH)

    loads[0].wait()
    loads[1].wait()
    for i in range(2):
        for h in range(2):
            arrived(x1.at[i, h], x_sem.at[2 * i + h])
            n = SEQ // 2
            project(x1[i, h].reshape(n, D), g1[...], w1, q_ref, kt_ref, v_ref, i, n * h, n)
        if i == 0:
            loads[2].wait()
            pl.semaphore_wait(known, COLS - 1)

            @pl.loop(0, 2)
            def _(step):
                part = lax.rem(step + chip, 2)
                row_block(0, 0, part)
                send_block(0, part, 0)

    @pl.loop(0, 2)
    def _(step):
        part = lax.rem(step + chip, 2)
        row_block(1, 0, part)
        send_block(0, part, 1)

    @pl.loop(0, 2)
    def _(step):
        part = lax.rem(step + chip, 2)

        @pl.loop(0, 2)
        def _(i):
            row_block(i, 1, part)

        send_block(1, part, None)

    for load in loads[3:]:
        load.wait()

    for h in range(2):
        arrived(here.at[h], h_sem.at[h])

        @pl.loop(0, ROWS // 4)
        def _(n):
            first = ROWS // 2 * h + 2 * n
            pair = [
                jnp.concatenate(
                    [
                        here[h, pl.ds((2 * n + m) * COLS, COLS), i].astype(F32).reshape(64, 128).astype(BF16)
                        for i in range(2)
                    ],
                    axis=0,
                )
                for m in range(2)
            ]
            cells = jnp.dot(pick[1], jnp.concatenate(pair, axis=1), preferred_element_type=F32).astype(BF16)
            for m in range(2):
                for f in range(4):
                    for j in range(2):
                        x2[j, pl.ds((first + m) * 16, 16), 128 * f : 128 * f + 128] = cells[
                            32 * f + 16 * j : 32 * f + 16 * j + 16, 128 * m : 128 * m + 128
                        ]

        for j in range(2 - h):
            n = SEQ // 2
            project(x2[j, n * h : n * h + n], g2[...], w2, q_ref, kt_ref, v_ref, j, n * h, n)

    for j in range(2):
        if j == 1:
            n = SEQ // 2
            project(x2[j, n:], g2[...], w2, q_ref, kt_ref, v_ref, j, n, n)

        @pl.loop(0, SEQ // QB)
        def _(step):
            block = lax.rem(step + place // 8, SEQ // QB)
            at = pl.multiple_of(block * QB, QB)
            mixed = attend(q_ref, kt_ref, v_ref, j, at)
            total = x2[j, pl.ds(at, QB), :].astype(F32) + jnp.dot(mixed, o2[...], preferred_element_type=F32)
            done[j, pl.ds(at, QB), :] = total.astype(BF16)

            def send(k):
                to_place = 8 * block + lax.rem(place + k, 8)
                to = 2 * lax.rem(to_place, 16) + to_place // 16
                src, dst = done.at[j, pl.ds(pl.multiple_of(16 * to_place, 16), 16)], back.at[2 * place + j]
                return to, src, dst, pltpu.make_async_remote_copy(
                    src, dst, b_sent, b_sem.at[place // 8], device_id=(to, c), device_id_type=MESH
                )

            to, src, dst, copy = send(0)

            @pl.when(to == r)
            def _():
                pltpu.make_async_copy(src, dst, b_sem.at[place // 8]).start()

            @pl.when(to != r)
            def _():
                copy.start()

            for k in (1, 7, 2, 6, 3, 5, 4):
                send(k)[-1].start()

    outs = []
    for g in range(4):
        arrived(back.at[pl.ds(16 * g, 16)], b_sem.at[g])
        cells = back[pl.ds(16 * g, 16)].reshape(256, D)
        cells = jnp.dot(pick3[...], cells, preferred_element_type=F32).astype(BF16)
        final[:, 16 * g : 16 * g + 16, :] = cells.reshape(16, 16, D)
        outs.append(
            pltpu.make_async_copy(
                final.at[:, pl.ds(16 * g, 16)], result_ref.at[:, pl.ds(16 * g, 16)], f_sem.at[g]
            )
        )
        outs[-1].start()

    for i in range(2):
        arrived(x1.at[i, :, pl.ds(0, COLS - 1)], x_sent.at[i])
    arrived(away.at[pl.ds(0, ROWS * COLS - 1)], h_sent)
    arrived(back.at[pl.ds(0, 2 * (ROWS - 1))], b_sent)
    for out in outs:
        out.wait()


def per_device(grid, gain_lon, qkv_lon, out_lon, gain_lat, qkv_lat, out_lat):
    place = pl.BlockSpec(memory_space=pltpu.HBM)
    dma = pltpu.SemaphoreType.DMA
    return pl.pallas_call(
        kernel,
        out_shape=jax.ShapeDtypeStruct((16, 64, D), BF16),
        in_specs=[place] * 7,
        out_specs=pl.BlockSpec(memory_space=pl.ANY),
        scratch_shapes=[
            pltpu.VMEM((1, D), F32),
            pltpu.VMEM((D, 3 * D), BF16),
            pltpu.VMEM((D, D), BF16),
            pltpu.VMEM((1, D), F32),
            pltpu.VMEM((D, 3 * D), BF16),
            pltpu.VMEM((D, D), BF16),
            pltpu.VMEM((2, 2, COLS, 32, D), BF16),
            pltpu.VMEM((2, SEQ, D), BF16),
            pltpu.VMEM((2, SEQ, D), BF16),
            pltpu.VMEM((2, D, SEQ), BF16),
            pltpu.VMEM((2, PAIRS, 2 * SEQ, 256), BF16),
            pltpu.VMEM((2, 128, 128), BF16),
            pltpu.VMEM((256, 256), BF16),
            pltpu.VMEM((ROWS * COLS, 2, 8, 128), BF16),
            pltpu.VMEM((2, ROWS * COLS // 2, 2, 8, 128), BF16),
            pltpu.VMEM((2, SEQ, D), BF16),
            pltpu.VMEM((64, 16, D), BF16),
            pltpu.VMEM((16, 64, D), BF16),
            dma((6,)),
            dma((4,)),
            dma((2,)),
            pltpu.SemaphoreType.REGULAR,
            pltpu.SemaphoreType.REGULAR,
            dma((2,)),
            dma,
            dma((4,)),
            dma,
            dma((4,)),
        ],
        compiler_params=pltpu.CompilerParams(
            collective_id=0, has_side_effects=True, vmem_limit_bytes=56 * 2**20
        ),
        cost_estimate=pl.CostEstimate(flops=6 * 10**9, bytes_accessed=8 * 2**20, transcendentals=8 * 2**20),
    )(grid.reshape(16, 2, 32, D), gain_lon.reshape(1, D), qkv_lon, out_lon, gain_lat.reshape(1, D), qkv_lat, out_lat)


def solution(mesh):
    return jax.shard_map(
        per_device,
        mesh=mesh,
        in_specs=(P("rows", "cols", None), P(), P(), P(), P(), P(), P()),
        out_specs=P("rows", "cols", None),
        check_vma=False,
    )
```

```python
import functools

import jax
import jax.numpy as jnp
from jax import lax
from jax.experimental import pallas as pl
from jax.experimental.pallas import tpu as pltpu
from jax.sharding import PartitionSpec as P

D = 512
PAIRS = 4
SEQ = 512
ROWS = 32
COLS = 8
QB = 128
SCALE = 64 ** (-0.5) * 1.4426950408889634
MESH = pl.DeviceIdType.MESH
BF16 = jnp.bfloat16
F32 = jnp.float32


def arrived(ref, sem):
    pltpu.make_async_copy(ref, ref, sem).wait()


def selection(n, source):
    out = lax.broadcasted_iota(jnp.int32, (n, n), 0)
    take = lax.broadcasted_iota(jnp.int32, (n, n), 1)
    return (take == source(out)).astype(F32).astype(BF16)


def norm(x, gain):
    scale = lax.rsqrt(jnp.mean(x * x, axis=-1, keepdims=True) + 1e-06)
    return (x * scale * gain).astype(BF16)


def project(x, gain, w_ref, q_ref, kt_ref, v_ref, line, at, n):
    normed = norm(x.astype(F32), gain)
    q = jnp.dot(normed, w_ref[:, :D], preferred_element_type=F32)
    q_ref[line, pl.ds(at, n), :] = (q * SCALE).astype(BF16)
    k = jnp.dot(normed, w_ref[:, D : 2 * D], preferred_element_type=F32)
    kt_ref[line, :, pl.ds(at, n)] = k.T.astype(BF16)
    v = jnp.dot(normed, w_ref[:, 2 * D :], preferred_element_type=F32)
    low = lax.broadcasted_iota(jnp.int32, (n, 128), 1) < 64
    for p in range(PAIRS):
        vp = v[:, 128 * p : 128 * p + 128]
        v_ref[line, p, pl.ds(at, n), :128] = jnp.where(low, vp, 0.0).astype(BF16)
        v_ref[line, p, pl.ds(SEQ + at, n), :128] = jnp.where(low, 0.0, vp).astype(BF16)


def attend(q_ref, kt_ref, v_ref, line, at):
    low = lax.broadcasted_iota(jnp.int32, (QB, 128), 1) < 64
    mixed = []
    for p in range(PAIRS):
        q = q_ref[line, pl.ds(at, QB), 128 * p : 128 * p + 128].astype(F32)
        both = jnp.concatenate([jnp.where(low, q, 0.0), jnp.where(low, 0.0, q)], axis=0).astype(BF16)
        scores = jnp.dot(both, kt_ref[line, 128 * p : 128 * p + 128, :], preferred_element_type=F32)
        weights = jnp.exp2(scores - jnp.max(scores, axis=-1, keepdims=True)).astype(BF16)
        weights = jnp.concatenate([weights[:QB], weights[QB:]], axis=1)
        total = jnp.dot(weights, v_ref[line, p], preferred_element_type=F32)
        mixed.append((total[:, :128] / total[:, 128:]).astype(BF16))
    return jnp.concatenate(mixed, axis=1)


def kernel(
    grid_ref, gain_lon, qkv_lon, out_lon, gain_lat, qkv_lat, out_lat, result_ref,
    g1, w1, o1, g2, w2, o2, x1, x2, q_ref, kt_ref, v_ref, pick, pick3, away, here, done, back, final,
    w_sem, x_sem, x_sent, met, known, h_sem, h_sent, b_sem, b_sent, f_sem,
):
    r, c = lax.axis_index("rows"), lax.axis_index("cols")
    core, chip = lax.rem(r, 2), r // 2
    place = core * 16 + chip
    loads = [
        pltpu.make_async_copy(src, dst, w_sem.at[n])
        for n, (src, dst) in enumerate(
            [(gain_lon, g1), (qkv_lon, w1), (out_lon, o1), (gain_lat, g2), (qkv_lat, w2), (out_lat, o2)]
        )
    ]
    for load in loads:
        load.start()

    barrier = pltpu.get_barrier_semaphore()

    @pl.loop(1, COLS)
    def _(k):
        pl.semaphore_signal(barrier, inc=1, device_id=(r, lax.rem(c + k, COLS)), device_id_type=MESH)

    four = [r + (1 - 2 * core), lax.rem(r + 16, ROWS), lax.rem(r + 16, ROWS) + (1 - 2 * core)]

    @pl.loop(1, 8)
    def _(k):
        to = r // 16 * 16 + lax.rem(r + 2 * k, 16)
        pl.semaphore_signal(barrier, inc=1, device_id=(to, c), device_id_type=MESH)

    for to in four:
        pl.semaphore_signal(barrier, inc=1, device_id=(to, c), device_id_type=MESH)

    pick[0] = selection(128, lambda o: (o % 8 // 2) * 32 + 2 * (o // 8) + o % 2)
    pick[1] = selection(128, lambda o: (o % 2) * 64 + (o % 16 // 2) * 8 + (o // 32) * 2 + o // 16 % 2)
    pick3[...] = selection(256, lambda o: (o % 16) * 16 + o // 16)
    ones = (lax.broadcasted_iota(jnp.int32, (SEQ, 128), 1) < 64).astype(F32)
    for line in range(2):
        for p in range(PAIRS):
            v_ref[line, p, :SEQ, 128:] = ones.astype(BF16)
            v_ref[line, p, SEQ:, 128:] = (1.0 - ones).astype(BF16)

    pl.semaphore_wait(barrier, 17)
    for to in four:
        pl.semaphore_signal(met, inc=1, device_id=(to, c), device_id_type=MESH)

    for i in range(2):
        for h in range(2):
            pltpu.make_async_copy(grid_ref.at[2 * c + i, h], x1.at[i, h, c], x_sem.at[2 * i + h]).start()

    def piece(i, h, q, k):
        to, cells = lax.rem(c + k, COLS), pl.ds(16 * q, 16)
        pltpu.make_async_remote_copy(
            grid_ref.at[2 * to + i, h, cells], x1.at[i, h, c, cells], x_sent.at[i], x_sem.at[2 * i + h],
            device_id=(r, to), device_id_type=MESH,
        ).start()

    for i, h in ((0, 0), (0, 1), (1, 0), (1, 1)):
        for q in range(2):
            for k in (1, 7, 2, 6, 3, 5, 4):
                piece(i, h, q, k)

    def row_block(i, to_core, part):
        block = 2 * to_core + part
        at = pl.multiple_of(block * QB, QB)
        mixed = attend(q_ref, kt_ref, v_ref, i, at)
        base = x1[i, to_core, pl.ds(4 * part, 4)].reshape(QB, D)
        first = base.astype(F32) + jnp.dot(mixed, o1[...], preferred_element_type=F32)
        first = first.astype(BF16)
        for g in range(QB // 32):
            cells = jnp.concatenate(
                [first[32 * g : 32 * g + 32, 128 * f : 128 * f + 128] for f in range(4)], axis=0
            )
            cells = jnp.dot(pick[0], cells, preferred_element_type=F32)
            away[pl.ds(block * (QB // 2) + 16 * g, 16), i] = cells.reshape(16, 8, 128).astype(BF16)

    def send_block(to_core, part, i):
        block = 2 * to_core + part

        def send(k, n):
            to_chip = lax.rem(chip + k, ROWS // 2)
            turn = lax.rem(c + n, 4)
            to = (2 * to_chip + to_core, 4 * part + turn)
            src, dst = away.at[64 * block + 16 * turn + to_chip], here.at[core, COLS * chip + c]
            if i is not None:
                src, dst = src.at[i], dst.at[i]
            return to, src, dst, pltpu.make_async_remote_copy(
                src, dst, h_sent, h_sem.at[core], device_id=to, device_id_type=MESH
            )

        @pl.loop(0, 4)
        def _(n):
            for k in (4, 12, 3, 13, 5, 11, 2, 14, 6, 10, 1, 15, 7, 9, 8):
                send(k, n)[-1].start()
            to, src, dst, copy = send(0, n)
            own = jnp.logical_and(to[0] == r, to[1] == c)

            @pl.when(own)
            def _():
                pltpu.make_async_copy(src, dst, h_sem.at[core]).start()

            @pl.when(jnp.logical_not(own))
            def _():
                copy.start()

    pl.semaphore_wait(met, 3)

    @pl.loop(1, COLS)
    def _(k):
        pl.semaphore_signal(known, inc=1, device_id=(r, lax.rem(c + k, COLS)), device_id_type=MESH)

    loads[0].wait()
    loads[1].wait()
    for i in range(2):
        for h in range(2):
            arrived(x1.at[i, h], x_sem.at[2 * i + h])
            n = SEQ // 2
            project(x1[i, h].reshape(n, D), g1[...], w1, q_ref, kt_ref, v_ref, i, n * h, n)
        if i == 0:
            loads[2].wait()
            pl.semaphore_wait(known, COLS - 1)

            @pl.loop(0, 2)
            def _(step):
                part = lax.rem(step + chip, 2)
                row_block(0, 0, part)
                send_block(0, part, 0)

    @pl.loop(0, 2)
    def _(step):
        part = lax.rem(step + chip, 2)
        row_block(1, 0, part)
        send_block(0, part, 1)

    @pl.loop(0, 2)
    def _(step):
        part = lax.rem(step + chip, 2)

        @pl.loop(0, 2)
        def _(i):
            row_block(i, 1, part)

        send_block(1, part, None)

    for load in loads[3:]:
        load.wait()

    for h in range(2):
        arrived(here.at[h], h_sem.at[h])

        @pl.loop(0, ROWS // 4)
        def _(n):
            first = ROWS // 2 * h + 2 * n
            pair = [
                jnp.concatenate(
                    [
                        here[h, pl.ds((2 * n + m) * COLS, COLS), i].astype(F32).reshape(64, 128).astype(BF16)
                        for i in range(2)
                    ],
                    axis=0,
                )
                for m in range(2)
            ]
            cells = jnp.dot(pick[1], jnp.concatenate(pair, axis=1), preferred_element_type=F32).astype(BF16)
            for m in range(2):
                for f in range(4):
                    for j in range(2):
                        x2[j, pl.ds((first + m) * 16, 16), 128 * f : 128 * f + 128] = cells[
                            32 * f + 16 * j : 32 * f + 16 * j + 16, 128 * m : 128 * m + 128
                        ]

        for j in range(2 - h):
            n = SEQ // 2
            project(x2[j, n * h : n * h + n], g2[...], w2, q_ref, kt_ref, v_ref, j, n * h, n)

    for j in range(2):
        if j == 1:
            n = SEQ // 2
            project(x2[j, n:], g2[...], w2, q_ref, kt_ref, v_ref, j, n, n)

        @pl.loop(0, SEQ // QB)
        def _(step):
            block = lax.rem(step + place // 8, SEQ // QB)
            at = pl.multiple_of(block * QB, QB)
            mixed = attend(q_ref, kt_ref, v_ref, j, at)
            total = x2[j, pl.ds(at, QB), :].astype(F32) + jnp.dot(mixed, o2[...], preferred_element_type=F32)
            done[j, pl.ds(at, QB), :] = total.astype(BF16)

            def send(k):
                to_place = 8 * block + lax.rem(place + k, 8)
                to = 2 * lax.rem(to_place, 16) + to_place // 16
                src, dst = done.at[j, pl.ds(pl.multiple_of(16 * to_place, 16), 16)], back.at[2 * place + j]
                return to, src, dst, pltpu.make_async_remote_copy(
                    src, dst, b_sent, b_sem.at[place // 8], device_id=(to, c), device_id_type=MESH
                )

            to, src, dst, copy = send(0)

            @pl.when(to == r)
            def _():
                pltpu.make_async_copy(src, dst, b_sem.at[place // 8]).start()

            @pl.when(to != r)
            def _():
                copy.start()

            for k in (4, 3, 5, 2, 6, 1, 7):
                send(k)[-1].start()

    outs = []
    for g in range(4):
        arrived(back.at[pl.ds(16 * g, 16)], b_sem.at[g])
        cells = back[pl.ds(16 * g, 16)].reshape(256, D)
        cells = jnp.dot(pick3[...], cells, preferred_element_type=F32).astype(BF16)
        final[:, 16 * g : 16 * g + 16, :] = cells.reshape(16, 16, D)
        outs.append(
            pltpu.make_async_copy(
                final.at[:, pl.ds(16 * g, 16)], result_ref.at[:, pl.ds(16 * g, 16)], f_sem.at[g]
            )
        )
        outs[-1].start()

    for i in range(2):
        arrived(x1.at[i, :, pl.ds(0, COLS - 1)], x_sent.at[i])
    arrived(away.at[pl.ds(0, ROWS * COLS - 1)], h_sent)
    arrived(back.at[pl.ds(0, 2 * (ROWS - 1))], b_sent)
    for out in outs:
        out.wait()


def per_device(grid, gain_lon, qkv_lon, out_lon, gain_lat, qkv_lat, out_lat):
    place = pl.BlockSpec(memory_space=pltpu.HBM)
    dma = pltpu.SemaphoreType.DMA
    return pl.pallas_call(
        kernel,
        out_shape=jax.ShapeDtypeStruct((16, 64, D), BF16),
        in_specs=[place] * 7,
        out_specs=pl.BlockSpec(memory_space=pl.ANY),
        scratch_shapes=[
            pltpu.VMEM((1, D), F32),
            pltpu.VMEM((D, 3 * D), BF16),
            pltpu.VMEM((D, D), BF16),
            pltpu.VMEM((1, D), F32),
            pltpu.VMEM((D, 3 * D), BF16),
            pltpu.VMEM((D, D), BF16),
            pltpu.VMEM((2, 2, COLS, 32, D), BF16),
            pltpu.VMEM((2, SEQ, D), BF16),
            pltpu.VMEM((2, SEQ, D), BF16),
            pltpu.VMEM((2, D, SEQ), BF16),
            pltpu.VMEM((2, PAIRS, 2 * SEQ, 256), BF16),
            pltpu.VMEM((2, 128, 128), BF16),
            pltpu.VMEM((256, 256), BF16),
            pltpu.VMEM((ROWS * COLS, 2, 8, 128), BF16),
            pltpu.VMEM((2, ROWS * COLS // 2, 2, 8, 128), BF16),
            pltpu.VMEM((2, SEQ, D), BF16),
            pltpu.VMEM((64, 16, D), BF16),
            pltpu.VMEM((16, 64, D), BF16),
            dma((6,)),
            dma((4,)),
            dma((2,)),
            pltpu.SemaphoreType.REGULAR,
            pltpu.SemaphoreType.REGULAR,
            dma((2,)),
            dma,
            dma((4,)),
            dma,
            dma((4,)),
        ],
        compiler_params=pltpu.CompilerParams(
            collective_id=0, has_side_effects=True, vmem_limit_bytes=56 * 2**20
        ),
        cost_estimate=pl.CostEstimate(flops=6 * 10**9, bytes_accessed=8 * 2**20, transcendentals=8 * 2**20),
    )(grid.reshape(16, 2, 32, D), gain_lon.reshape(1, D), qkv_lon, out_lon, gain_lat.reshape(1, D), qkv_lat, out_lat)


def solution(mesh):
    return jax.shard_map(
        per_device,
        mesh=mesh,
        in_specs=(P("rows", "cols", None), P(), P(), P(), P(), P(), P()),
        out_specs=P("rows", "cols", None),
        check_vma=False,
    )
```
